256 devices in a mesh: subtree: 16 (over z, core), front: 16 (over x, y).
Axes of the slice: x: 4, y: 4, z: 8, core: 2. Of those that a mesh axis runs over, the one named last changes fastest.
Arguments:
- leaf_rhs: float32 [16, 2048, 256], P('subtree', 'front'), may hold values from -6 to 6
- mid_rhs: float32 [4, 4096, 256], P(None, 'front'), may hold values from -6 to 6
- root_rhs: float32 [10240, 256], P('front'), may hold values from -6 to 6
- leaf_lower: float32 [16, 2048, 2048], P('subtree', None, 'front'), may hold values from -0.125 to 0.125
- leaf_below: float32 [16, 2048, 2048], P('subtree', None, 'front'), may hold values from -0.125 to 0.125
- leaf_right: float32 [16, 2048, 2048], P('subtree', None, 'front'), may hold values from -0.125 to 0.125
- leaf_upper: float32 [16, 2048, 2048], P('subtree', None, 'front'), may hold values from -0.125 to 0.125
- mid_lower: float32 [4, 4096, 4096], P(None, 'subtree', 'front'), may hold values from -0.09375 to 0.09375
- mid_below: float32 [4, 4096, 4096], P(None, 'front', 'subtree'), may hold values from -0.09375 to 0.09375
- mid_right: float32 [4, 4096, 4096], P(None, 'subtree', 'front'), may hold values from -0.09375 to 0.09375
- mid_upper: float32 [4, 4096, 4096], P(None, 'front', 'subtree'), may hold values from -0.09375 to 0.09375
- root_lower: float32 [10240, 10240], P('subtree', 'front'), may hold values from -0.0625 to 0.0625
- root_upper: float32 [10240, 10240], P('front', 'subtree'), may hold values from -0.0625 to 0.0625
- leaf_parent: int32 [16], replicated, may hold values from 0 to 3, as said below
- leaf_sizes: int32 [16], replicated, may hold values from 1024 to 2048, as said below
- leaf_map: int32 [16, 16], replicated, may hold values from 0 to 63, as said below
- mid_map: int32 [4, 32], replicated, may hold values from 0 to 79, as said below
Outputs:
- leaf_sol: float32 [16, 2048, 256], P('subtree', 'front')
- mid_sol: float32 [4, 4096, 256], P(None, 'front')
- root_sol: float32 [10240, 256], P('front')
The draws below stay inside these ranges and needn't reach their ends.
Inputs may be any that keep to these rules, and one draw needn't show every extreme that they name: `leaf_parent`: every level-1 front is the parent of at least one lowest-level front. `leaf_sizes`: a multiple of 128; some front has all 2048 rows live. `leaf_map`: a front's blocks go to distinct parent blocks; update block b of a lowest-level front, with c = b, goes to c * 2 + i or to that plus 4096 / 128, for some i with 0 <= i < 2. `mid_map`: a front's blocks go to distinct root blocks; update block b of a level-1 front, with c = b // 2, goes to c * 5 + i for some i with 0 <= i < 5.
All inputs are finite; a program needn't handle non-finite values.
Results may differ from the reference program's by a relative error of at most 0.00013.
Values sent between devices are 32-bit elements; how exact they have to be, the bound alone decides.
A program may use at most 64 MiB of HBM per device.

```python
import jax
import jax.numpy as jnp
from jax import lax

LEAF_PIV = 2048
MID_PIV = 4096
ROOT_ORD = 10240
BLOCK = 128
SCEN = 256
LEAVES = 16
MIDS = 4
LEAF_SPAN = 1
MID_SPAN = 2
ROOT_SPAN = 5


def draw_leaf_parent(key, part):
    base = jax.random.randint(key, (LEAVES,), 0, MIDS)
    order = jax.random.permutation(jax.random.fold_in(key, 7), LEAVES)
    chosen = order[:MIDS]
    return base.at[chosen].set(jnp.arange(MIDS, dtype=jnp.int32)).astype(jnp.int32)


def draw_leaf_sizes(key, part):
    counts = jax.random.randint(key, (LEAVES,), LEAF_PIV // (2 * BLOCK), LEAF_PIV // BLOCK + 1)
    chosen = jax.random.randint(jax.random.fold_in(key, 3), (), 0, LEAVES)
    counts = counts.at[chosen].set(LEAF_PIV // BLOCK)
    return (counts * BLOCK).astype(jnp.int32)


def draw_leaf_map(key, part):
    columns = LEAF_PIV // BLOCK // LEAF_SPAN
    keys = jax.random.split(key, LEAVES * columns)

    def pick_one(single):
        return jax.random.permutation(single, 2 * MID_SPAN)[:LEAF_SPAN].astype(jnp.int32)
    picks = jax.vmap(pick_one)(keys).reshape(LEAVES, columns, LEAF_SPAN)
    steps_up = jnp.arange(LEAF_SPAN, dtype=jnp.int32)
    picks = picks.at[0, 0].set(steps_up)
    picks = picks.at[LEAVES - 1, columns - 1].set(2 * MID_SPAN - 1 - steps_up)
    halves = picks // MID_SPAN
    within = picks % MID_SPAN
    column = jnp.arange(columns, dtype=jnp.int32)[None, :, None]
    blocks = halves * (MID_PIV // BLOCK) + column * MID_SPAN + within
    return blocks.reshape(LEAVES, LEAF_PIV // BLOCK).astype(jnp.int32)


def draw_mid_map(key, part):
    columns = MID_PIV // BLOCK // MID_SPAN
    keys = jax.random.split(key, MIDS * columns)

    def pick_one(single):
        return jax.random.permutation(single, ROOT_SPAN)[:MID_SPAN].astype(jnp.int32)
    picks = jax.vmap(pick_one)(keys).reshape(MIDS, columns, MID_SPAN)
    steps_up = jnp.arange(MID_SPAN, dtype=jnp.int32)
    picks = picks.at[0, 0].set(steps_up)
    picks = picks.at[MIDS - 1, columns - 1].set(ROOT_SPAN - 1 - steps_up)
    column = jnp.arange(columns, dtype=jnp.int32)[None, :, None]
    blocks = column * ROOT_SPAN + picks
    return blocks.reshape(MIDS, MID_PIV // BLOCK).astype(jnp.int32)


def block_scale(own_key, dims, cuts, low, high):
    def one(position, parts):
        steps = jax.random.uniform(jax.random.fold_in(jax.random.fold_in(own_key, 6), position), (parts,), jnp.float32, low / len(cuts), high / len(cuts))
        return jnp.repeat(jnp.exp(steps), dims[position] // parts).reshape((-1,) + (1,) * (len(dims) - position - 1))

    loudness = one(*cuts[0])
    for cut in cuts[1:]:
        loudness = loudness * one(*cut)
    return loudness


def scatter_about(key, shape, scale, reach, shards=(), kind=jnp.bfloat16):
    level = block_scale(key, shape, shards, -0.22, 0.18) if shards else 1.0
    result = jax.random.normal(key, shape, jnp.float32) * scale * level
    return jnp.minimum(jnp.maximum(result, -reach), reach).astype(kind)


def setup_inputs(seed: int = 0) -> dict:
    arg_keys = jax.random.split(jax.random.key(seed), 18)
    leaf_rhs = scatter_about(arg_keys[0], (LEAVES, LEAF_PIV, SCEN), 1.0, 6.0, ((0, 16), (1, 16)), jnp.float32)
    mid_rhs = scatter_about(arg_keys[1], (MIDS, MID_PIV, SCEN), 1.0, 6.0, ((1, 16),), jnp.float32)
    root_rhs = scatter_about(arg_keys[2], (ROOT_ORD, SCEN), 1.0, 6.0, ((0, 16),), jnp.float32)
    leaf_lower = scatter_about(arg_keys[3], (LEAVES, LEAF_PIV, LEAF_PIV), LEAF_PIV ** -0.5, 0.125, ((0, 16), (2, 16)), jnp.float32)
    leaf_below = scatter_about(arg_keys[4], (LEAVES, LEAF_PIV, LEAF_PIV), LEAF_PIV ** -0.5, 0.125, ((0, 16), (2, 16)), jnp.float32)
    leaf_right = scatter_about(arg_keys[5], (LEAVES, LEAF_PIV, LEAF_PIV), LEAF_PIV ** -0.5, 0.125, ((0, 16), (2, 16)), jnp.float32)
    leaf_upper = scatter_about(arg_keys[6], (LEAVES, LEAF_PIV, LEAF_PIV), LEAF_PIV ** -0.5, 0.125, ((0, 16), (2, 16)), jnp.float32)
    mid_lower = scatter_about(arg_keys[7], (MIDS, MID_PIV, MID_PIV), MID_PIV ** -0.5, 0.09375, ((1, 16), (2, 16)), jnp.float32)
    mid_below = scatter_about(arg_keys[8], (MIDS, MID_PIV, MID_PIV), MID_PIV ** -0.5, 0.09375, ((1, 16), (2, 16)), jnp.float32)
    mid_right = scatter_about(arg_keys[9], (MIDS, MID_PIV, MID_PIV), MID_PIV ** -0.5, 0.09375, ((1, 16), (2, 16)), jnp.float32)
    mid_upper = scatter_about(arg_keys[10], (MIDS, MID_PIV, MID_PIV), MID_PIV ** -0.5, 0.09375, ((1, 16), (2, 16)), jnp.float32)
    root_lower = scatter_about(arg_keys[11], (ROOT_ORD, ROOT_ORD), ROOT_ORD ** -0.5, 0.0625, ((0, 16), (1, 16)), jnp.float32)
    root_upper = scatter_about(arg_keys[12], (ROOT_ORD, ROOT_ORD), ROOT_ORD ** -0.5, 0.0625, ((0, 16), (1, 16)), jnp.float32)
    leaf_parent = draw_leaf_parent(jax.random.fold_in(arg_keys[17], 71), 0)
    leaf_sizes = draw_leaf_sizes(jax.random.fold_in(arg_keys[17], 71), 0)
    leaf_map = draw_leaf_map(jax.random.fold_in(arg_keys[17], 71), 0)
    mid_map = draw_mid_map(jax.random.fold_in(arg_keys[17], 71), 0)
    return {"leaf_rhs": leaf_rhs, "mid_rhs": mid_rhs, "root_rhs": root_rhs, "leaf_lower": leaf_lower, "leaf_below": leaf_below, "leaf_right": leaf_right, "leaf_upper": leaf_upper, "mid_lower": mid_lower, "mid_below": mid_below, "mid_right": mid_right, "mid_upper": mid_upper, "root_lower": root_lower, "root_upper": root_upper, "leaf_parent": leaf_parent, "leaf_sizes": leaf_sizes, "leaf_map": leaf_map, "mid_map": mid_map}


def batched(matrix, vector):
    return jnp.einsum('fab,fbr->far', matrix.astype(jnp.float32), vector.astype(jnp.float32), precision=lax.Precision.HIGHEST)


def reference(leaf_rhs, mid_rhs, root_rhs, leaf_lower, leaf_below, leaf_right, leaf_upper, mid_lower, mid_below, mid_right, mid_upper, root_lower, root_upper, leaf_parent, leaf_sizes, leaf_map, mid_map):
    positions = jnp.arange(LEAF_PIV, dtype=jnp.int32)
    live = (positions[None, :] < leaf_sizes[:, None]).astype(jnp.float32)[:, :, None]
    leaf_fwd = live * batched(leaf_lower, live * leaf_rhs)
    leaf_contrib = -batched(leaf_below, leaf_fwd)
    mid_blocks = 2 * MID_PIV // BLOCK
    mid_front = jnp.zeros((MIDS, mid_blocks, BLOCK, SCEN), jnp.float32)
    mid_front = mid_front.at[leaf_parent[:, None], leaf_map].add(leaf_contrib.reshape(LEAVES, LEAF_PIV // BLOCK, BLOCK, SCEN))
    mid_front = mid_front.reshape(MIDS, 2 * MID_PIV, SCEN)
    mid_fwd = batched(mid_lower, mid_rhs + mid_front[:, :MID_PIV])
    mid_contrib = mid_front[:, MID_PIV:] - batched(mid_below, mid_fwd)
    root_blocks = jnp.zeros((ROOT_ORD // BLOCK, BLOCK, SCEN), jnp.float32)
    root_blocks = root_blocks.at[mid_map].add(mid_contrib.reshape(MIDS, MID_PIV // BLOCK, BLOCK, SCEN))
    root_start = root_rhs + root_blocks.reshape(ROOT_ORD, SCEN)
    root_fwd = jnp.dot(root_lower, root_start, preferred_element_type=jnp.float32, precision=lax.Precision.HIGHEST)
    root_sol = jnp.dot(root_upper, root_fwd, preferred_element_type=jnp.float32, precision=lax.Precision.HIGHEST)
    mid_ext = root_sol.reshape(ROOT_ORD // BLOCK, BLOCK, SCEN)[mid_map].reshape(MIDS, MID_PIV, SCEN)
    mid_sol = batched(mid_upper, mid_fwd - batched(mid_right, mid_ext))
    whole_mid = jnp.concatenate([mid_sol, mid_ext], axis=1).reshape(MIDS, mid_blocks, BLOCK, SCEN)
    leaf_ext = whole_mid[leaf_parent[:, None], leaf_map].reshape(LEAVES, LEAF_PIV, SCEN)
    leaf_sol = live * batched(leaf_upper, live * (leaf_fwd - batched(leaf_right, leaf_ext)))
    return leaf_sol, mid_sol, root_sol
```

```python
import types

import jax
import jax.numpy as jnp
from jax import lax
from jax.experimental import pallas as pl
from jax.experimental.pallas import tpu as pltpu
from jax.sharding import PartitionSpec as P

MESH = pl.DeviceIdType.MESH
F32 = jnp.float32
BF16 = jnp.bfloat16
LANES = 128
FRONT_LEAF = ((0, 64), (1024, 64))
FRONT_MID = ((0, 32), (512, 32))
FRONT_ROOT = ((0, 24), (384, 16))

MATRICES = (
    (2048, 128),
    (2048, 128),
    (4, 256, 256),
    (4, 256, 256),
    (640, 640),
    (640, 640),
    (4, 256, 256),
    (4, 256, 256),
    (2048, 128),
    (2048, 128),
)
LEAF_LOWER, LEAF_BELOW, MID_LOWER, MID_BELOW, ROOT_LOWER = range(5)
ROOT_UPPER, MID_RIGHT, MID_UPPER, LEAF_RIGHT, LEAF_UPPER = range(5, 10)


def vmem(*shape):
    return pltpu.VMEM(shape, F32)


def front_scratch(layout):
    return [dict(r1=vmem(3, 4 * unit, LANES), r2=vmem(3, unit, LANES)) for _, unit in layout]


def exchange_scratch(layout):
    return [dict(r1=vmem(3, 4 * unit, LANES), r2=vmem(4, 4 * unit, LANES)) for _, unit in layout]


def subtree_scratch(blocks):
    return dict(core=vmem(8, blocks, 8, LANES), ring=vmem(7, blocks, 8, LANES))


def chain_scratch():
    return dict(
        part=vmem(2048, LANES),
        zpart8=vmem(16, 8, 8, LANES),
        zpart5=vmem(16, 5, 8, LANES),
        leaf_fwd=vmem(128, LANES),
        contrib=vmem(16, 8, LANES),
        children=vmem(16, 8, LANES),
        update=vmem(8, 8, LANES),
        pivot=vmem(16, 8, 8, LANES),
        mid_fwd=vmem(1024, LANES),
        start=vmem(16, 5, 8, LANES),
        root_fwd=vmem(640, LANES),
        root_sol=vmem(16, 5, 8, LANES),
        mid_back=vmem(1024, LANES),
        mid_sol=vmem(16, 8, 8, LANES),
        p1=front_scratch(FRONT_LEAF),
        p2=front_scratch(FRONT_LEAF),
        x4=exchange_scratch(FRONT_MID),
        z5=subtree_scratch(8),
        x6=exchange_scratch(FRONT_ROOT),
        z7=subtree_scratch(5),
        x8=exchange_scratch(FRONT_MID),
        z9=subtree_scratch(8),
        p10=front_scratch(FRONT_LEAF),
        p11=front_scratch(FRONT_LEAF),
        x=pltpu.VMEM((2048, 256), BF16),
    )


SCRATCH = dict(
    raw=[vmem(*shape) for shape in MATRICES],
    split=[pltpu.VMEM(shape[:-1] + (2 * shape[-1],), BF16) for shape in MATRICES],
    leaf_rhs=vmem(128, 256),
    mid_rhs=vmem(8, 8, 256),
    root_rhs=vmem(5, 8, 256),
    out_leaf=vmem(128, 256),
    out_mid=vmem(8, 16, 8, 256),
    out_root=vmem(5, 16, 8, 256),
    chains=[chain_scratch(), chain_scratch()],
)
SHAPES, TREE = jax.tree.flatten(SCRATCH)
SEMS = 512
ORDER = (0, 0, 1, 0, 1, 0, 1, 0, 0, 1, 0, 1, 0, 1, 0, 0, 1, 1, 0, 0, 1, 1, 0, 1, 0, 1, 0, 0, 1, 0, 1, 0, 1, 0, 1, 0, 1, 0, 1, 0, 1, 0, 1, 0, 1, 1, 0, 0, 1, 1, 0, 1, 1, 0, 0, 1, 0, 1, 1, 1, 0, 1, 0, 1, 1, 0)


def named(tree):
    if isinstance(tree, dict):
        return types.SimpleNamespace(**{key: named(value) for key, value in tree.items()})
    if isinstance(tree, list):
        return [named(value) for value in tree]
    return tree


def split(value):
    high = value.astype(BF16)
    low = (value - high.astype(F32)).astype(BF16)
    return high, low


def kernel(*refs):
    leaf_rhs_ref, mid_rhs_ref, root_rhs_ref = refs[:3]
    matrix_refs = refs[3:13]
    parent_ref, sizes_ref, leaf_map_ref, mid_map_ref = refs[13:17]
    out_leaf, out_mid, out_root = refs[17:20]
    scratch = named(jax.tree.unflatten(TREE, refs[20 : 20 + len(SHAPES)]))
    send_sems, recv_sems, load_sems, out_sems = refs[20 + len(SHAPES) :]

    s = lax.axis_index("subtree")
    f = lax.axis_index("front")
    xi, yi = f // 4, f % 4
    zi, ci = s // 2, s % 2
    rank = ci * 8 + zi

    def device(dx=0, dy=0, dz=0, dc=0):
        return (
            ((zi + dz) % 8) * 2 + (ci + dc) % 2,
            ((xi + dx) % 4) * 4 + (yi + dy) % 4,
        )

    def load(index, src, dst):
        copy = pltpu.make_async_copy(src, dst, load_sems.at[index])
        copy.start()
        return copy

    load_leaf_rhs = load(10, leaf_rhs_ref, scratch.leaf_rhs)
    loads = [load(0, matrix_refs[0], scratch.raw[0])]

    barrier = pltpu.get_barrier_semaphore()
    partners = [device(dx=d) for d in (1, 2, 3)] + [device(dy=d) for d in (1, 2, 3)]
    partners += [device(dz=d, dc=c) for d in range(8) for c in range(2) if (d, c) != (0, 0)]
    for partner in partners:
        pl.semaphore_signal(barrier, inc=1, device_id=partner, device_id_type=MESH)

    loads[0].wait()
    loads += [load(i, matrix_refs[i], scratch.raw[i]) for i in range(1, 10)]
    load_mid_rhs = load(11, mid_rhs_ref.at[:, rank], scratch.mid_rhs)
    load_root_rhs = load(12, root_rhs_ref.at[:, rank], scratch.root_rhs)

    def cast(name):
        if name != LEAF_LOWER:
            loads[name].wait()
        src, dst = scratch.raw[name], scratch.split[name]
        width = src.shape[-1]
        if len(src.shape) == 3:

            def body(i, carry):
                high, low = split(src[i])
                dst[i, :, 0:width] = high
                dst[i, :, width : 2 * width] = low
                return carry

            lax.fori_loop(0, src.shape[0], body, 0)
        else:
            tile = 256 if width == 128 else 64

            def body(i, carry):
                rows = pl.ds(pl.multiple_of(i * tile, tile), tile)
                high, low = split(src[rows, :])
                dst[rows, 0:width] = high
                dst[rows, width : 2 * width] = low
                return carry

            lax.fori_loop(0, src.shape[0] // tile, body, 0)

    counter = [0]
    first_send = [True]

    def chain(h):
        mine = scratch.chains[h]
        lanes = slice(h * LANES, (h + 1) * LANES)
        pending = []

        def send(src, dst, target):
            if first_send[0]:
                pl.semaphore_wait(barrier, len(partners))
                first_send[0] = False
            index = counter[0]
            counter[0] += 1
            copy = pltpu.make_async_remote_copy(
                src_ref=src,
                dst_ref=dst,
                send_sem=send_sems.at[index],
                recv_sem=recv_sems.at[index],
                device_id=target,
                device_id_type=MESH,
            )
            copy.start()
            pending.append(copy)
            return copy

        def flush():
            for copy in pending:
                copy.wait_send()
            pending.clear()

        def arrive(copies):
            for copy in copies:
                copy.wait_recv()

        def put_x(row, value):
            depth = value.shape[0]
            high, low = split(value)
            x = mine.x
            for r in (row, row + depth):
                x[r : r + depth, 0:LANES] = high
                x[r : r + depth, LANES : 2 * LANES] = low

        def dot(a, b):
            both = jnp.dot(a, b, preferred_element_type=F32)
            return both[:, :LANES] + both[:, LANES:]

        def position(half):
            return (xi, yi) if half == 0 else (yi, xi)

        def along(half, primary, d):
            use_x = (half == 0) == primary
            return device(dx=d) if use_x else device(dy=d)

        def front_scatter(bufs, layout):
            part = mine.part
            copies = []
            for half, (base, unit) in enumerate(layout):
                ia, ib = position(half)
                got = bufs[half].r1
                mineset = []
                for d in (2, 1, 3):
                    to = (ia + d) % 4
                    rows = pl.ds(pl.multiple_of(base + to * (4 * unit), 8), 4 * unit)
                    mineset.append(send(part.at[rows], got.at[d - 1], along(half, True, d)))
                copies.append(mineset)
            yield
            second = []
            for half, (base, unit) in enumerate(layout):
                ia, ib = position(half)
                got = bufs[half].r1
                arrive(copies[half])
                own = pl.multiple_of(base + ia * (4 * unit), 8)
                rows = pl.ds(own, 4 * unit)
                part[rows, :] = (part[rows, :] + got[0]) + (got[1] + got[2])
                got2 = bufs[half].r2
                mineset = []
                for d in (2, 1, 3):
                    to = (ib + d) % 4
                    rows = pl.ds(pl.multiple_of(own + to * unit, 8), unit)
                    mineset.append(send(part.at[rows], got2.at[d - 1], along(half, False, d)))
                second.append(mineset)
            yield
            sums = []
            for half, (base, unit) in enumerate(layout):
                ia, ib = position(half)
                got2 = bufs[half].r2
                arrive(second[half])
                rows = pl.ds(pl.multiple_of(base + ia * (4 * unit) + ib * unit, 8), unit)
                sums.append((part[rows, :] + got2[0]) + (got2[1] + got2[2]))
            return sums

        def front_reduce(bufs, layout, full, minuend=None):
            part = mine.part
            first = []
            for half, (base, unit) in enumerate(layout):
                ia, _ = position(half)
                copies = []
                for d in (2, 1, 3):
                    to = (ia + d) % 4
                    rows = pl.ds(pl.multiple_of(base + to * (4 * unit), 8), 4 * unit)
                    copies.append(send(part.at[rows], bufs[half].r1.at[d - 1], along(half, True, d)))
                first.append(copies)
            yield
            second = []
            for half, (base, unit) in enumerate(layout):
                ia, ib = position(half)
                got, got2 = bufs[half].r1, bufs[half].r2
                arrive(first[half])
                rows = pl.ds(pl.multiple_of(base + ia * (4 * unit), 8), 4 * unit)
                got2[ib] = (part[rows, :] + got[0]) + (got[1] + got[2])
                second.append(
                    [send(got2.at[ib], got2.at[ib], along(half, False, d)) for d in (2, 1, 3)]
                )
            yield
            last = []
            for half, (base, unit) in enumerate(layout):
                ia, _ = position(half)
                got2 = bufs[half].r2
                arrive(second[half])
                rows = pl.ds(pl.multiple_of(base + ia * (4 * unit), 8), 4 * unit)
                total = (got2[0] + got2[1]) + (got2[2] + got2[3])
                full[rows, :] = total if minuend is None else minuend[rows, :] - total
                last.append(
                    [send(full.at[rows], full.at[rows], along(half, True, d)) for d in (2, 1, 3)]
                )
            yield
            for copies in last:
                arrive(copies)

        def subtree_scatter(bufs, zpart):
            got = bufs.core
            theirs = pl.ds(pl.multiple_of((1 - ci) * 8, 8), 8)
            copy = send(zpart.at[theirs], got, device(dc=1))
            yield
            arrive([copy])
            start = pl.multiple_of(ci * 8, 8)
            zpart[pl.ds(start, 8)] = zpart[pl.ds(start, 8)] + got[...]
            ring = bufs.ring
            copies = []
            for d in (4, 3, 5, 2, 6, 1, 7):
                to = (zi + d) % 8
                copies.append(send(zpart.at[start + to], ring.at[d - 1], device(dz=d)))
            yield
            arrive(copies)
            a = (ring[0] + ring[1]) + (ring[2] + ring[3])
            b = (ring[4] + ring[5]) + (ring[6] + zpart[rank])
            return a + b

        def subtree_gather(full, chunk):
            full[rank] = chunk
            near = (1, 7, 2, 6, 3, 5, 4)
            copies = {d: send(full.at[rank], full.at[rank], device(dz=d)) for d in reversed(near)}
            across = [send(full.at[rank], full.at[rank], device(dc=1))]
            yield
            for d in near:
                arrive([copies[d]])
                slot = ci * 8 + (zi + 8 - d) % 8
                across.append(send(full.at[slot], full.at[slot], device(dc=1)))
            yield
            arrive(across)

        def leaf_product(name):
            flush()
            part, x, a = mine.part, mine.x, scratch.split[name]

            def body(j, carry):
                rows = pl.ds(pl.multiple_of(j * 256, 256), 256)
                y = dot(a[rows, :], x[0:256, :])
                for k in range(2):
                    block = 2 * j + k
                    low = pl.multiple_of(block * 64, 64)
                    high = pl.multiple_of(1024 + ((block % 4) * 4 + block // 4) * 64, 64)
                    part[pl.ds(low, 64), :] = y[k * 128 : k * 128 + 64]
                    part[pl.ds(high, 64), :] = y[k * 128 + 64 : k * 128 + 128]
                return carry

            lax.fori_loop(0, 8, body, 0)

        def mid_product(name, across_subtree):
            flush()
            x, a = mine.x, scratch.split[name]

            def body(p, carry):
                y = dot(a[p], x[pl.ds(pl.multiple_of(p * 512, 512), 512), :])
                if across_subtree:
                    y = y.reshape(2, 16, 8, LANES)
                    mine.zpart8[:, 2 * p] = y[0]
                    mine.zpart8[:, 2 * p + 1] = y[1]
                else:
                    mine.part[pl.ds(pl.multiple_of(p * 256, 256), 256), :] = y
                return carry

            lax.fori_loop(0, 4, body, 0)

        def root_product(name, across_subtree):
            flush()
            x, a = mine.x, scratch.split[name]

            def body(q, carry):
                rows = pl.ds(pl.multiple_of(q * 128, 128), 128)
                y = dot(a[rows, :], x[0:1280, :])
                if across_subtree:
                    mine.zpart5[:, q] = y.reshape(16, 8, LANES)
                else:
                    mine.part[rows, :] = y
                return carry

            lax.fori_loop(0, 5, body, 0)

        def block_of(full, t):
            return full[:, t].reshape(128, LANES)

        def root_slot(p, k):
            return jnp.clip(mid_map_ref[p, 2 * f + k] - 5 * f, 0, 4)

        positions = f * 128 + lax.broadcasted_iota(jnp.int32, (128, LANES), 0)
        live = (positions < sizes_ref[s]).astype(F32)
        lead = h == 0

        if lead:
            load_leaf_rhs.wait()
            cast(LEAF_LOWER)
        put_x(0, live * scratch.leaf_rhs[:, lanes])
        leaf_product(LEAF_LOWER)
        stage = front_scatter(mine.p1, FRONT_LEAF)
        next(stage)
        if lead:
            cast(LEAF_BELOW)
        yield
        sums = yield from stage
        leaf_fwd = live * jnp.concatenate(sums, axis=0)
        mine.leaf_fwd[...] = leaf_fwd

        put_x(0, leaf_fwd)
        leaf_product(LEAF_BELOW)
        stage = front_scatter(mine.p2, FRONT_LEAF)
        next(stage)
        if lead:
            cast(MID_LOWER)
        yield
        sums = yield from stage
        contrib = -jnp.concatenate(sums, axis=0)

        mine.contrib[...] = contrib.reshape(16, 8, LANES)
        children = mine.children
        children[s] = mine.contrib[rank]
        copies = []
        for d in (4, 3, 5, 2, 6, 1, 7, 0):
            for c in range(2):
                if (d, c) != (0, 0):
                    to = ((ci + c) % 2) * 8 + (zi + d) % 8
                    copies.append(send(mine.contrib.at[to], children.at[s], device(dz=d, dc=c)))
        if lead:
            cast(MID_BELOW)
            load_mid_rhs.wait()
        yield
        arrive(copies)
        placed = [jnp.zeros((8, LANES), F32) for _ in range(16)]
        for g in range(16):
            block = leaf_map_ref[g, f]
            upper = block >= 32
            slot = block - 2 * f - jnp.where(upper, 32, 0)
            target = parent_ref[g] * 4 + jnp.where(upper, 2, 0) + slot
            value = children[g]
            for t in range(16):
                placed[t] = placed[t] + jnp.where(target == t, value, 0.0)
        rhs = scratch.mid_rhs
        pivot = [rhs[t, :, lanes] + placed[(t // 2) * 4 + t % 2] for t in range(8)]
        mine.update[...] = jnp.stack([placed[(t // 2) * 4 + 2 + t % 2] for t in range(8)])
        yield from subtree_gather(mine.pivot, jnp.stack(pivot))

        for p in range(4):
            full = mine.pivot
            put_x(512 * p, jnp.concatenate([block_of(full, 2 * p), block_of(full, 2 * p + 1)], axis=0))
        mid_product(MID_LOWER, False)
        stage = front_reduce(mine.x4, FRONT_MID, mine.mid_fwd)
        next(stage)
        if lead:
            cast(ROOT_LOWER)
        yield
        yield from stage

        for p in range(4):
            put_x(512 * p, mine.mid_fwd[256 * p : 256 * p + 256, :])
        mid_product(MID_BELOW, True)
        stage = subtree_scatter(mine.z5, mine.zpart8)
        next(stage)
        yield
        next(stage)
        if lead:
            cast(ROOT_UPPER)
            load_root_rhs.wait()
        yield
        chunk = mine.update[...] - (yield from stage)
        start = [scratch.root_rhs[q, :, lanes] for q in range(5)]
        for p in range(4):
            for k in range(2):
                slot = mid_map_ref[p, 2 * f + k] - 5 * f
                for q in range(5):
                    start[q] = start[q] + jnp.where(slot == q, chunk[2 * p + k], 0.0)
        yield from subtree_gather(mine.start, jnp.stack(start))

        put_x(0, jnp.concatenate([block_of(mine.start, q) for q in range(5)], axis=0))
        root_product(ROOT_LOWER, False)
        stage = front_reduce(mine.x6, FRONT_ROOT, mine.root_fwd)
        next(stage)
        if lead:
            cast(MID_RIGHT)
        yield
        yield from stage

        put_x(0, mine.root_fwd[...])
        root_product(ROOT_UPPER, True)
        stage = subtree_scatter(mine.z7, mine.zpart5)
        next(stage)
        yield
        next(stage)
        if lead:
            cast(MID_UPPER)
        yield
        chunk = yield from stage
        yield from subtree_gather(mine.root_sol, chunk)

        for p in range(4):
            ext = [
                block_of(mine.root_sol, root_slot(p, k)) for k in range(2)
            ]
            put_x(512 * p, jnp.concatenate(ext, axis=0))
        mid_product(MID_RIGHT, False)
        stage = front_reduce(mine.x8, FRONT_MID, mine.mid_back, mine.mid_fwd)
        next(stage)
        if lead:
            cast(LEAF_RIGHT)
        for q in range(5):
            scratch.out_root[q, :, :, lanes] = mine.root_sol[:, q]
        yield
        yield from stage

        for p in range(4):
            put_x(512 * p, mine.mid_back[256 * p : 256 * p + 256, :])
        mid_product(MID_UPPER, True)
        stage = subtree_scatter(mine.z9, mine.zpart8)
        next(stage)
        yield
        next(stage)
        if lead:
            cast(LEAF_UPPER)
        yield
        chunk = yield from stage
        yield from subtree_gather(mine.mid_sol, chunk)

        block = leaf_map_ref[s, f]
        p = parent_ref[s]
        upper = block >= 32
        slot = jnp.clip(block - 2 * f - jnp.where(upper, 32, 0), 0, 1)
        from_sol = block_of(mine.mid_sol, 2 * p + slot)
        from_ext = block_of(mine.root_sol, root_slot(p, slot))
        put_x(0, jnp.where(upper, from_ext, from_sol))
        leaf_product(LEAF_RIGHT)
        stage = front_scatter(mine.p10, FRONT_LEAF)
        next(stage)
        for t in range(8):
            scratch.out_mid[t, :, :, lanes] = mine.mid_sol[:, t]
        yield
        sums = yield from stage
        put_x(0, live * (mine.leaf_fwd[...] - jnp.concatenate(sums, axis=0)))

        leaf_product(LEAF_UPPER)
        sums = yield from front_scatter(mine.p11, FRONT_LEAF)
        scratch.out_leaf[:, lanes] = live * jnp.concatenate(sums, axis=0)
        flush()

    chains = [chain(0), chain(1)]
    for which in ORDER:
        next(chains[which], None)

    outs = [
        pltpu.make_async_copy(scratch.out_leaf, out_leaf, out_sems.at[0]),
        pltpu.make_async_copy(scratch.out_mid, out_mid, out_sems.at[1]),
        pltpu.make_async_copy(scratch.out_root, out_root, out_sems.at[2]),
    ]
    for copy in outs:
        copy.start()
    for copy in outs:
        copy.wait()


def on_device(
    leaf_rhs,
    mid_rhs,
    root_rhs,
    leaf_lower,
    leaf_below,
    leaf_right,
    leaf_upper,
    mid_lower,
    mid_below,
    mid_right,
    mid_upper,
    root_lower,
    root_upper,
    leaf_parent,
    leaf_sizes,
    leaf_map,
    mid_map,
):
    operands = [leaf_rhs[0], mid_rhs.reshape(8, 16, 8, 256), root_rhs.reshape(5, 16, 8, 256)]
    operands += [leaf_lower[0], leaf_below[0], mid_lower, mid_below, root_lower]
    operands += [root_upper, mid_right, mid_upper, leaf_right[0], leaf_upper[0]]
    anywhere = pl.BlockSpec(memory_space=pl.ANY)
    scalars = pl.BlockSpec(memory_space=pltpu.SMEM)
    leaf_sol, mid_sol, root_sol = pl.pallas_call(
        kernel,
        out_shape=(
            jax.ShapeDtypeStruct((128, 256), F32),
            jax.ShapeDtypeStruct((8, 16, 8, 256), F32),
            jax.ShapeDtypeStruct((5, 16, 8, 256), F32),
        ),
        in_specs=[anywhere] * len(operands) + [scalars] * 4,
        out_specs=(anywhere,) * 3,
        scratch_shapes=SHAPES
        + [
            pltpu.SemaphoreType.DMA((SEMS,)),
            pltpu.SemaphoreType.DMA((SEMS,)),
            pltpu.SemaphoreType.DMA((13,)),
            pltpu.SemaphoreType.DMA((3,)),
        ],
        compiler_params=pltpu.CompilerParams(
            collective_id=0, has_side_effects=True, vmem_limit_bytes=60 * 2**20
        ),
        name="solve",
    )(*operands, leaf_parent, leaf_sizes, leaf_map, mid_map)
    return leaf_sol[None], mid_sol.reshape(4, 256, 256), root_sol.reshape(640, 256)


def solution(mesh):
    return jax.shard_map(
        on_device,
        mesh=mesh,
        in_specs=(
            P("subtree", "front", None),
            P(None, "front", None),
            P("front", None),
            P("subtree", None, "front"),
            P("subtree", None, "front"),
            P("subtree", None, "front"),
            P("subtree", None, "front"),
            P(None, "subtree", "front"),
            P(None, "front", "subtree"),
            P(None, "subtree", "front"),
            P(None, "front", "subtree"),
            P("subtree", "front"),
            P("front", "subtree"),
            P(),
            P(),
            P(),
            P(),
        ),
        out_specs=(P("subtree", "front", None), P(None, "front", None), P("front", None)),
        check_vma=False,
    )
```

```python
import types

import jax
import jax.numpy as jnp
from jax import lax
from jax.experimental import pallas as pl
from jax.experimental.pallas import tpu as pltpu
from jax.sharding import PartitionSpec as P

MESH = pl.DeviceIdType.MESH
F32 = jnp.float32
BF16 = jnp.bfloat16
LANES = 128
FRONT_LEAF = ((0, 64), (1024, 64))
FRONT_MID = ((0, 32), (512, 32))
FRONT_ROOT = ((0, 24), (384, 16))

MATRICES = (
    (2048, 128),
    (2048, 128),
    (4, 256, 256),
    (4, 256, 256),
    (640, 640),
    (640, 640),
    (4, 256, 256),
    (4, 256, 256),
    (2048, 128),
    (2048, 128),
)
LEAF_LOWER, LEAF_BELOW, MID_LOWER, MID_BELOW, ROOT_LOWER = range(5)
ROOT_UPPER, MID_RIGHT, MID_UPPER, LEAF_RIGHT, LEAF_UPPER = range(5, 10)


def vmem(*shape):
    return pltpu.VMEM(shape, F32)


def front_scratch(layout):
    return [dict(relay=vmem(2, 2 * unit, LANES), r1=vmem(2, 4 * unit, LANES), r2=vmem(3, unit, LANES)) for _, unit in layout]


def exchange_scratch(layout):
    return [dict(r1=vmem(3, 4 * unit, LANES), r2=vmem(4, 4 * unit, LANES)) for _, unit in layout]


def subtree_scratch(blocks):
    return dict(core=vmem(8, blocks, 8, LANES), ring=vmem(7, blocks, 8, LANES))


def chain_scratch():
    return dict(
        part=vmem(2048, LANES),
        zpart8=vmem(16, 8, 8, LANES),
        zpart5=vmem(16, 5, 8, LANES),
        leaf_fwd=vmem(128, LANES),
        contrib=vmem(16, 8, LANES),
        children=vmem(16, 8, LANES),
        update=vmem(8, 8, LANES),
        pivot=vmem(16, 8, 8, LANES),
        mid_fwd=vmem(1024, LANES),
        start=vmem(16, 5, 8, LANES),
        root_fwd=vmem(640, LANES),
        root_sol=vmem(16, 5, 8, LANES),
        mid_back=vmem(1024, LANES),
        mid_sol=vmem(16, 8, 8, LANES),
        mid_own=vmem(8, 8, LANES),
        picked=vmem(16, 8, LANES),
        leaf_ext=vmem(16, 8, LANES),
        p1=front_scratch(FRONT_LEAF),
        p2=front_scratch(FRONT_LEAF),
        x4=exchange_scratch(FRONT_MID),
        z5=subtree_scratch(8),
        x6=exchange_scratch(FRONT_ROOT),
        z7=subtree_scratch(5),
        x8=exchange_scratch(FRONT_MID),
        z9=subtree_scratch(8),
        p10=front_scratch(FRONT_LEAF),
        p11=front_scratch(FRONT_LEAF),
        x=pltpu.VMEM((2048, 256), BF16),
    )


SCRATCH = dict(
    raw=[vmem(*shape) for shape in MATRICES],
    split=[pltpu.VMEM(shape[:-1] + (2 * shape[-1],), BF16) for shape in MATRICES],
    leaf_rhs=vmem(128, 256),
    mid_rhs=vmem(8, 8, 256),
    root_rhs=vmem(5, 8, 256),
    out_leaf=vmem(128, 256),
    out_mid=vmem(8, 16, 8, 256),
    out_root=vmem(5, 16, 8, 256),
    chains=[chain_scratch(), chain_scratch()],
)
SHAPES, TREE = jax.tree.flatten(SCRATCH)
SEMS = 576
ORDER = (0, 0, 1, 0, 1, 0, 1, 0, 0, 1, 0, 1, 0, 1, 0, 1, 0, 1, 0, 0, 1, 1, 0, 0, 1, 1, 0, 1, 0, 1, 0, 0, 1, 0, 1, 0, 1, 0, 1, 0, 1, 0, 1, 0, 1, 0, 1, 0, 1, 1, 0, 0, 1, 1, 0, 1, 0, 1, 0, 1, 0, 1, 1, 0, 1, 0, 1, 0, 1, 1, 0, 1)


def named(tree):
    if isinstance(tree, dict):
        return types.SimpleNamespace(**{key: named(value) for key, value in tree.items()})
    if isinstance(tree, list):
        return [named(value) for value in tree]
    return tree


def split(value):
    high = value.astype(BF16)
    low = (value - high.astype(F32)).astype(BF16)
    return high, low


def kernel(*refs):
    leaf_rhs_ref, mid_rhs_ref, root_rhs_ref = refs[:3]
    matrix_refs = refs[3:13]
    parent_ref, sizes_ref, leaf_map_ref, mid_map_ref = refs[13:17]
    out_leaf, out_mid, out_root = refs[17:20]
    scratch = named(jax.tree.unflatten(TREE, refs[20 : 20 + len(SHAPES)]))
    send_sems, recv_sems, load_sems, out_sems = refs[20 + len(SHAPES) :]

    s = lax.axis_index("subtree")
    f = lax.axis_index("front")
    xi, yi = f // 4, f % 4
    zi, ci = s // 2, s % 2
    rank = ci * 8 + zi

    def device(dx=0, dy=0, dz=0, dc=0):
        return (
            ((zi + dz) % 8) * 2 + (ci + dc) % 2,
            ((xi + dx) % 4) * 4 + (yi + dy) % 4,
        )

    def load(index, src, dst):
        copy = pltpu.make_async_copy(src, dst, load_sems.at[index])
        copy.start()
        return copy

    load_leaf_rhs = load(10, leaf_rhs_ref, scratch.leaf_rhs)
    quarters = [pl.ds(512 * i, 512) for i in range(4)]
    firsts = [
        load(13 + i, matrix_refs[0].at[rows], scratch.raw[0].at[rows])
        for i, rows in enumerate(quarters)
    ]

    barrier = pltpu.get_barrier_semaphore()
    partners = [device(dx=d) for d in (1, 2, 3)] + [device(dy=d) for d in (1, 2, 3)]
    partners += [device(dz=d, dc=c) for d in range(8) for c in range(2) if (d, c) != (0, 0)]
    for partner in partners:
        pl.semaphore_signal(barrier, inc=1, device_id=partner, device_id_type=MESH)

    for copy in firsts:
        copy.wait()
    loads = [None] + [load(i, matrix_refs[i], scratch.raw[i]) for i in range(1, 10)]
    load_mid_rhs = load(11, mid_rhs_ref.at[:, rank], scratch.mid_rhs)
    load_root_rhs = load(12, root_rhs_ref.at[:, rank], scratch.root_rhs)

    def cast(name):
        if name != LEAF_LOWER:
            loads[name].wait()
        src, dst = scratch.raw[name], scratch.split[name]
        width = src.shape[-1]
        if len(src.shape) == 3:

            def body(i, carry):
                high, low = split(src[i])
                dst[i, :, 0:width] = high
                dst[i, :, width : 2 * width] = low
                return carry

            lax.fori_loop(0, src.shape[0], body, 0)
        else:
            tile = 256 if width == 128 else 64

            def body(i, carry):
                rows = pl.ds(pl.multiple_of(i * tile, tile), tile)
                high, low = split(src[rows, :])
                dst[rows, 0:width] = high
                dst[rows, width : 2 * width] = low
                return carry

            lax.fori_loop(0, src.shape[0] // tile, body, 0)

    outputs, ready = [], []

    def output(index, src, dst):
        copy = pltpu.make_async_copy(src, dst, out_sems.at[index])
        copy.start()
        outputs.append(copy)

    counter = [0]
    first_send = [True]

    def chain(h):
        mine = scratch.chains[h]
        lanes = slice(h * LANES, (h + 1) * LANES)
        pending = []

        late = []

        def send(src, dst, target, kept=True):
            if first_send[0]:
                pl.semaphore_wait(barrier, len(partners))
                first_send[0] = False
            index = counter[0]
            counter[0] += 1
            copy = pltpu.make_async_remote_copy(
                src_ref=src,
                dst_ref=dst,
                send_sem=send_sems.at[index],
                recv_sem=recv_sems.at[index],
                device_id=target,
                device_id_type=MESH,
            )
            copy.start()
            (late if kept else pending).append(copy)
            return copy

        def flush():
            for copy in pending:
                copy.wait_send()
            pending.clear()

        def flush_late():
            for copy in late:
                copy.wait_send()
            late.clear()

        def arrive(copies):
            for copy in copies:
                copy.wait_recv()

        def put_x(row, value):
            depth = value.shape[0]
            high, low = split(value)
            x = mine.x
            for r in (row, row + depth):
                x[r : r + depth, 0:LANES] = high
                x[r : r + depth, LANES : 2 * LANES] = low

        def dot(a, b):
            both = jnp.dot(a, b, preferred_element_type=F32)
            return both[:, :LANES] + both[:, LANES:]

        def position(half):
            return (xi, yi) if half == 0 else (yi, xi)

        def along(half, primary, d):
            use_x = (half == 0) == primary
            return device(dx=d) if use_x else device(dy=d)

        def front_scatter(bufs, layout):
            part = mine.part

            def rows_of(half, to, upper):
                base, unit = layout[half]
                return pl.ds(pl.multiple_of(base + to * (4 * unit) + 2 * unit * upper, 8), 2 * unit)

            relayed, straight, summed = [], [], []
            for half, (base, unit) in enumerate(layout):
                ia, _ = position(half)
                copies = []
                for side, d in ((0, 1), (1, 3)):
                    rows = rows_of(half, (ia + 2) % 4, side)
                    copies.append(send(part.at[rows], bufs[half].relay.at[side], along(half, True, d), False))
                relayed.append(copies)
            for half, (base, unit) in enumerate(layout):
                ia, _ = position(half)
                copies = []
                for side, d in ((0, 1), (1, 3)):
                    rows = rows_of(half, (ia + d) % 4, 1 - side)
                    there = pl.ds(2 * unit * (1 - side), 2 * unit)
                    copies.append(
                        send(part.at[rows], bufs[half].r1.at[side, there], along(half, True, d), False)
                    )
                straight.append(copies)
            yield
            for half, (base, unit) in enumerate(layout):
                ia, _ = position(half)
                copies = []
                for side, d in ((0, 1), (1, 3)):
                    arrive([relayed[half][side]])
                    rows = rows_of(half, (ia + d) % 4, side)
                    part[rows, :] = part[rows, :] + bufs[half].relay[side]
                    there = pl.ds(2 * unit * side, 2 * unit)
                    copies.append(
                        send(part.at[rows], bufs[half].r1.at[side, there], along(half, True, d), False)
                    )
                summed.append(copies)
            yield
            second = []
            for half, (base, unit) in enumerate(layout):
                ia, ib = position(half)
                got = bufs[half].r1
                arrive(straight[half])
                arrive(summed[half])
                own = pl.multiple_of(base + ia * (4 * unit), 8)
                rows = pl.ds(own, 4 * unit)
                part[rows, :] = part[rows, :] + (got[0] + got[1])
                got2 = bufs[half].r2
                mineset = []
                for d in (2, 1, 3):
                    to = (ib + d) % 4
                    rows = pl.ds(pl.multiple_of(own + to * unit, 8), unit)
                    mineset.append(send(part.at[rows], got2.at[d - 1], along(half, False, d), False))
                second.append(mineset)
            yield
            sums = []
            for half, (base, unit) in enumerate(layout):
                ia, ib = position(half)
                got2 = bufs[half].r2
                arrive(second[half])
                rows = pl.ds(pl.multiple_of(base + ia * (4 * unit) + ib * unit, 8), unit)
                sums.append((part[rows, :] + got2[0]) + (got2[1] + got2[2]))
            return sums

        def front_reduce(bufs, layout, full, minuend=None):
            part = mine.part
            first = []
            for half, (base, unit) in enumerate(layout):
                ia, _ = position(half)
                copies = []
                for d in (2, 1, 3):
                    to = (ia + d) % 4
                    rows = pl.ds(pl.multiple_of(base + to * (4 * unit), 8), 4 * unit)
                    copies.append(send(part.at[rows], bufs[half].r1.at[d - 1], along(half, True, d), False))
                first.append(copies)
            yield
            second = []
            for half, (base, unit) in enumerate(layout):
                ia, ib = position(half)
                got, got2 = bufs[half].r1, bufs[half].r2
                arrive(first[half])
                rows = pl.ds(pl.multiple_of(base + ia * (4 * unit), 8), 4 * unit)
                got2[ib] = (part[rows, :] + got[0]) + (got[1] + got[2])
                second.append(
                    [send(got2.at[ib], got2.at[ib], along(half, False, d)) for d in (2, 1, 3)]
                )
            yield
            last = []
            for half, (base, unit) in enumerate(layout):
                ia, _ = position(half)
                got2 = bufs[half].r2
                arrive(second[half])
                rows = pl.ds(pl.multiple_of(base + ia * (4 * unit), 8), 4 * unit)
                total = (got2[0] + got2[1]) + (got2[2] + got2[3])
                full[rows, :] = total if minuend is None else minuend[rows, :] - total
                last.append(
                    [send(full.at[rows], full.at[rows], along(half, True, d)) for d in (2, 1, 3)]
                )
            yield
            for copies in last:
                arrive(copies)

        def subtree_scatter(bufs, zpart):
            got = bufs.core
            theirs = pl.ds(pl.multiple_of((1 - ci) * 8, 8), 8)
            copy = send(zpart.at[theirs], got, device(dc=1), False)
            yield
            arrive([copy])
            start = pl.multiple_of(ci * 8, 8)
            zpart[pl.ds(start, 8)] = zpart[pl.ds(start, 8)] + got[...]
            ring = bufs.ring
            copies = []
            for d in (4, 3, 5, 2, 6, 1, 7):
                to = (zi + d) % 8
                copies.append(send(zpart.at[start + to], ring.at[d - 1], device(dz=d), False))
            yield
            arrive(copies)
            a = (ring[0] + ring[1]) + (ring[2] + ring[3])
            b = (ring[4] + ring[5]) + (ring[6] + zpart[rank])
            return a + b

        def subtree_gather(full, chunk):
            full[rank] = chunk
            near = (1, 7, 2, 6, 3, 5, 4)
            copies = {d: send(full.at[rank], full.at[rank], device(dz=d)) for d in reversed(near)}
            across = [send(full.at[rank], full.at[rank], device(dc=1))]
            yield
            for d in near:
                arrive([copies[d]])
                slot = ci * 8 + (zi + 8 - d) % 8
                across.append(send(full.at[slot], full.at[slot], device(dc=1)))
            yield
            arrive(across)

        def leaf_product(name):
            flush()
            part = mine.part
            y = dot(scratch.split[name][...], mine.x[0:256, :])
            for block in range(16):
                low, high = block * 64, 1024 + ((block % 4) * 4 + block // 4) * 64
                part[low : low + 64, :] = y[block * 128 : block * 128 + 64]
                part[high : high + 64, :] = y[block * 128 + 64 : block * 128 + 128]

        def mid_product(name, across_subtree):
            flush()
            x, a = mine.x, scratch.split[name]
            for p in range(4):
                y = dot(a[p], x[512 * p : 512 * p + 512, :])
                if across_subtree:
                    y = y.reshape(2, 16, 8, LANES)
                    mine.zpart8[:, 2 * p] = y[0]
                    mine.zpart8[:, 2 * p + 1] = y[1]
                else:
                    mine.part[256 * p : 256 * p + 256, :] = y

        def root_product(name, across_subtree):
            flush()
            y = dot(scratch.split[name][...], mine.x[0:1280, :])
            if across_subtree:
                for q in range(5):
                    mine.zpart5[:, q] = y[128 * q : 128 * q + 128].reshape(16, 8, LANES)
            else:
                mine.part[0:640, :] = y

        def block_of(full, t):
            return full[:, t].reshape(128, LANES)

        def root_slot(p, k):
            return jnp.clip(mid_map_ref[p, 2 * f + k] - 5 * f, 0, 4)

        positions = f * 128 + lax.broadcasted_iota(jnp.int32, (128, LANES), 0)
        live = (positions < sizes_ref[s]).astype(F32)
        lead = h == 0

        if lead:
            load_leaf_rhs.wait()
            cast(LEAF_LOWER)
        put_x(0, live * scratch.leaf_rhs[:, lanes])
        leaf_product(LEAF_LOWER)
        stage = front_scatter(mine.p1, FRONT_LEAF)
        next(stage)
        if lead:
            cast(LEAF_BELOW)
        yield
        sums = yield from stage
        leaf_fwd = live * jnp.concatenate(sums, axis=0)
        mine.leaf_fwd[...] = leaf_fwd

        put_x(0, leaf_fwd)
        leaf_product(LEAF_BELOW)
        stage = front_scatter(mine.p2, FRONT_LEAF)
        next(stage)
        if lead:
            cast(MID_LOWER)
        yield
        sums = yield from stage
        contrib = -jnp.concatenate(sums, axis=0)

        mine.contrib[...] = contrib.reshape(16, 8, LANES)
        children = mine.children
        children[s] = mine.contrib[rank]
        copies = []
        for d in (4, 3, 5, 2, 6, 1, 7, 0):
            for c in range(2):
                if (d, c) != (0, 0):
                    to = ((ci + c) % 2) * 8 + (zi + d) % 8
                    copies.append(send(mine.contrib.at[to], children.at[s], device(dz=d, dc=c)))
        if lead:
            cast(MID_BELOW)
            load_mid_rhs.wait()
        yield
        arrive(copies)
        placed = [jnp.zeros((8, LANES), F32) for _ in range(16)]
        for g in range(16):
            block = leaf_map_ref[g, f]
            upper = block >= 32
            slot = block - 2 * f - jnp.where(upper, 32, 0)
            target = parent_ref[g] * 4 + jnp.where(upper, 2, 0) + slot
            value = children[g]
            for t in range(16):
                placed[t] = placed[t] + jnp.where(target == t, value, 0.0)
        rhs = scratch.mid_rhs
        pivot = [rhs[t, :, lanes] + placed[(t // 2) * 4 + t % 2] for t in range(8)]
        mine.update[...] = jnp.stack([placed[(t // 2) * 4 + 2 + t % 2] for t in range(8)])
        yield from subtree_gather(mine.pivot, jnp.stack(pivot))

        for p in range(4):
            full = mine.pivot
            put_x(512 * p, jnp.concatenate([block_of(full, 2 * p), block_of(full, 2 * p + 1)], axis=0))
        mid_product(MID_LOWER, False)
        stage = front_reduce(mine.x4, FRONT_MID, mine.mid_fwd)
        next(stage)
        if lead:
            cast(ROOT_LOWER)
        yield
        yield from stage

        for p in range(4):
            put_x(512 * p, mine.mid_fwd[256 * p : 256 * p + 256, :])
        mid_product(MID_BELOW, True)
        stage = subtree_scatter(mine.z5, mine.zpart8)
        next(stage)
        yield
        next(stage)
        if lead:
            cast(ROOT_UPPER)
            load_root_rhs.wait()
        yield
        chunk = mine.update[...] - (yield from stage)
        start = [scratch.root_rhs[q, :, lanes] for q in range(5)]
        for p in range(4):
            for k in range(2):
                slot = mid_map_ref[p, 2 * f + k] - 5 * f
                for q in range(5):
                    start[q] = start[q] + jnp.where(slot == q, chunk[2 * p + k], 0.0)
        yield from subtree_gather(mine.start, jnp.stack(start))

        put_x(0, jnp.concatenate([block_of(mine.start, q) for q in range(5)], axis=0))
        root_product(ROOT_LOWER, False)
        stage = front_reduce(mine.x6, FRONT_ROOT, mine.root_fwd)
        next(stage)
        if lead:
            cast(MID_RIGHT)
        yield
        yield from stage

        put_x(0, mine.root_fwd[...])
        root_product(ROOT_UPPER, True)
        stage = subtree_scatter(mine.z7, mine.zpart5)
        next(stage)
        yield
        next(stage)
        if lead:
            cast(MID_UPPER)
        yield
        chunk = yield from stage
        yield from subtree_gather(mine.root_sol, chunk)

        for p in range(4):
            ext = [
                block_of(mine.root_sol, root_slot(p, k)) for k in range(2)
            ]
            put_x(512 * p, jnp.concatenate(ext, axis=0))
        mid_product(MID_RIGHT, False)
        stage = front_reduce(mine.x8, FRONT_MID, mine.mid_back, mine.mid_fwd)
        next(stage)
        if lead:
            cast(LEAF_RIGHT)
        for q in range(5):
            scratch.out_root[q, :, :, lanes] = mine.root_sol[:, q]
        ready.append(8)
        if ready.count(8) == 2:
            output(2, scratch.out_root, out_root)
        yield
        yield from stage

        for p in range(4):
            put_x(512 * p, mine.mid_back[256 * p : 256 * p + 256, :])
        mid_product(MID_UPPER, True)
        stage = subtree_scatter(mine.z9, mine.zpart8)
        next(stage)
        yield
        next(stage)
        if lead:
            cast(LEAF_UPPER)
        yield
        mine.mid_own[...] = yield from stage

        def leaf_target(g):
            block = leaf_map_ref[g, f]
            upper = block >= 32
            return parent_ref[g], jnp.clip(block - 2 * f - jnp.where(upper, 32, 0), 0, 1), upper

        for g in range(16):
            p, slot, _ = leaf_target(g)
            mine.picked[g] = mine.mid_own[2 * p + slot]
        mine.leaf_ext[rank] = mine.picked[s]
        copies = []
        for d in (4, 3, 5, 2, 6, 1, 7, 0):
            for c in range(2):
                if (d, c) != (0, 0):
                    to = ((zi + d) % 8) * 2 + (ci + c) % 2
                    copies.append(
                        send(mine.picked.at[to], mine.leaf_ext.at[rank], device(dz=d, dc=c))
                    )
        gather = subtree_gather(mine.mid_sol, mine.mid_own[...])
        next(gather)
        yield
        arrive(copies)

        p, slot, upper = leaf_target(s)
        from_sol = mine.leaf_ext[...].reshape(128, LANES)
        from_ext = block_of(mine.root_sol, root_slot(p, slot))
        put_x(0, jnp.where(upper, from_ext, from_sol))
        leaf_product(LEAF_RIGHT)
        stage = front_scatter(mine.p10, FRONT_LEAF)
        next(stage)
        yield
        next(stage)
        next(gather)
        yield
        sums = yield from stage
        put_x(0, live * (mine.leaf_fwd[...] - jnp.concatenate(sums, axis=0)))

        leaf_product(LEAF_UPPER)
        stage = front_scatter(mine.p11, FRONT_LEAF)
        next(stage)
        next(gather, None)
        for t in range(8):
            scratch.out_mid[t, :, :, lanes] = mine.mid_sol[:, t]
        ready.append(10)
        if ready.count(10) == 2:
            output(1, scratch.out_mid, out_mid)
        flush_late()
        yield
        sums = yield from stage
        scratch.out_leaf[:, lanes] = live * jnp.concatenate(sums, axis=0)
        flush()
        flush_late()

    chains = [chain(0), chain(1)]
    for which in ORDER:
        next(chains[which], None)

    output(0, scratch.out_leaf, out_leaf)
    for copy in outputs:
        copy.wait()


def copy_kernel(a, b, c, a_out, b_out, c_out, a_held, b_held, c_held, sems):
    steps = ((b, b_held, b_out), (c, c_held, c_out), (a, a_held, a_out))
    reads = [pltpu.make_async_copy(x, y, sems.at[i]) for i, (x, y, _) in enumerate(steps)]
    writes = [pltpu.make_async_copy(y, z, sems.at[3 + i]) for i, (_, y, z) in enumerate(steps)]
    for copy in reads:
        copy.start()
    for read, write in zip(reads, writes):
        read.wait()
        write.start()
    for copy in writes:
        copy.wait()


def on_device(
    leaf_rhs,
    mid_rhs,
    root_rhs,
    leaf_lower,
    leaf_below,
    leaf_right,
    leaf_upper,
    mid_lower,
    mid_below,
    mid_right,
    mid_upper,
    root_lower,
    root_upper,
    leaf_parent,
    leaf_sizes,
    leaf_map,
    mid_map,
):
    operands = [leaf_rhs[0], mid_rhs.reshape(8, 16, 8, 256), root_rhs.reshape(5, 16, 8, 256)]
    operands += [leaf_lower[0], leaf_below[0], mid_lower, mid_below, root_lower]
    operands += [root_upper, mid_right, mid_upper, leaf_right[0], leaf_upper[0]]
    anywhere = pl.BlockSpec(memory_space=pl.ANY)
    scalars = pl.BlockSpec(memory_space=pltpu.SMEM)
    shapes = (
        jax.ShapeDtypeStruct((128, 256), F32),
        jax.ShapeDtypeStruct((8, 16, 8, 256), F32),
        jax.ShapeDtypeStruct((5, 16, 8, 256), F32),
    )
    results = pl.pallas_call(
        kernel,
        out_shape=shapes,
        in_specs=[anywhere] * len(operands) + [scalars] * 4,
        out_specs=(anywhere,) * 3,
        scratch_shapes=SHAPES
        + [
            pltpu.SemaphoreType.DMA((SEMS,)),
            pltpu.SemaphoreType.DMA((SEMS,)),
            pltpu.SemaphoreType.DMA((17,)),
            pltpu.SemaphoreType.DMA((3,)),
        ],
        compiler_params=pltpu.CompilerParams(
            collective_id=0, has_side_effects=True, vmem_limit_bytes=60 * 2**20
        ),
        name="solve",
    )(*operands, leaf_parent, leaf_sizes, leaf_map, mid_map)
    leaf_sol, mid_sol, root_sol = pl.pallas_call(
        copy_kernel,
        out_shape=shapes,
        in_specs=[anywhere] * 3,
        out_specs=(anywhere,) * 3,
        scratch_shapes=[pltpu.VMEM(shape.shape, F32) for shape in shapes]
        + [pltpu.SemaphoreType.DMA((6,))],
    )(*results)
    return leaf_sol[None], mid_sol.reshape(4, 256, 256), root_sol.reshape(640, 256)


def solution(mesh):
    return jax.shard_map(
        on_device,
        mesh=mesh,
        in_specs=(
            P("subtree", "front", None),
            P(None, "front", None),
            P("front", None),
            P("subtree", None, "front"),
            P("subtree", None, "front"),
            P("subtree", None, "front"),
            P("subtree", None, "front"),
            P(None, "subtree", "front"),
            P(None, "front", "subtree"),
            P(None, "subtree", "front"),
            P(None, "front", "subtree"),
            P("subtree", "front"),
            P("front", "subtree"),
            P(),
            P(),
            P(),
            P(),
        ),
        out_specs=(P("subtree", "front", None), P(None, "front", None), P("front", None)),
        check_vma=False,
    )
```

```python
import types

import jax
import jax.numpy as jnp
from jax import lax
from jax.experimental import pallas as pl
from jax.experimental.pallas import tpu as pltpu
from jax.sharding import PartitionSpec as P

MESH = pl.DeviceIdType.MESH
F32 = jnp.float32
BF16 = jnp.bfloat16
LANES = 128
FRONT_LEAF = ((0, 64), (1024, 64))
FRONT_MID = ((0, 32), (512, 32))
FRONT_ROOT = ((0, 24), (384, 16))

MATRICES = (
    (2048, 128),
    (2048, 128),
    (4, 256, 256),
    (4, 256, 256),
    (640, 640),
    (640, 640),
    (4, 256, 256),
    (4, 256, 256),
    (2048, 128),
    (2048, 128),
)
LEAF_LOWER, LEAF_BELOW, MID_LOWER, MID_BELOW, ROOT_LOWER = range(5)
ROOT_UPPER, MID_RIGHT, MID_UPPER, LEAF_RIGHT, LEAF_UPPER = range(5, 10)


def vmem(*shape):
    return pltpu.VMEM(shape, F32)


def front_scratch(layout):
    return [dict(relay=vmem(2, 2 * unit, LANES), r1=vmem(2, 4 * unit, LANES), r2=vmem(3, unit, LANES)) for _, unit in layout]


def exchange_scratch(layout):
    return [dict(r1=vmem(3, 4 * unit, LANES), r2=vmem(4, 4 * unit, LANES)) for _, unit in layout]


def subtree_scratch(blocks):
    return dict(core=vmem(8, blocks, 8, LANES), ring=vmem(7, blocks, 8, LANES))


def chain_scratch():
    return dict(
        part=vmem(2048, LANES),
        zpart8=vmem(16, 8, 8, LANES),
        zpart5=vmem(16, 5, 8, LANES),
        leaf_fwd=vmem(128, LANES),
        contrib=vmem(16, 8, LANES),
        children=vmem(16, 8, LANES),
        update=vmem(8, 8, LANES),
        pivot=vmem(16, 8, 8, LANES),
        mid_fwd=vmem(1024, LANES),
        start=vmem(16, 5, 8, LANES),
        root_fwd=vmem(640, LANES),
        root_sol=vmem(16, 5, 8, LANES),
        mid_back=vmem(1024, LANES),
        mid_sol=vmem(16, 8, 8, LANES),
        mid_own=vmem(8, 8, LANES),
        picked=vmem(16, 8, LANES),
        leaf_ext=vmem(16, 8, LANES),
        p1=front_scratch(FRONT_LEAF),
        p2=front_scratch(FRONT_LEAF),
        x4=exchange_scratch(FRONT_MID),
        z5=subtree_scratch(8),
        x6=exchange_scratch(FRONT_ROOT),
        z7=subtree_scratch(5),
        x8=exchange_scratch(FRONT_MID),
        z9=subtree_scratch(8),
        p10=front_scratch(FRONT_LEAF),
        p11=front_scratch(FRONT_LEAF),
        x=pltpu.VMEM((2048, 256), BF16),
    )


SCRATCH = dict(
    raw=[vmem(*shape) for shape in MATRICES],
    split=[pltpu.VMEM(shape[:-1] + (2 * shape[-1],), BF16) for shape in MATRICES],
    leaf_rhs=vmem(128, 256),
    mid_rhs=vmem(8, 8, 256),
    root_rhs=vmem(5, 8, 256),
    out_leaf=vmem(128, 256),
    out_mid=vmem(8, 16, 8, 256),
    out_root=vmem(5, 16, 8, 256),
    chains=[chain_scratch(), chain_scratch()],
)
SHAPES, TREE = jax.tree.flatten(SCRATCH)
SEMS = 576
ORDER = (0, 0, 1, 0, 0, 1, 0, 1, 0, 1, 0, 1, 0, 1, 0, 1, 0, 1, 0, 0, 1, 1, 0, 0, 1, 1, 0, 1, 0, 1, 0, 0, 1, 0, 1, 0, 1, 0, 1, 0, 1, 0, 1, 0, 1, 0, 1, 0, 1, 1, 0, 0, 1, 1, 0, 1, 0, 1, 1, 0, 0, 1, 1, 0, 1, 0, 1, 0, 1, 1, 0, 1)


def named(tree):
    if isinstance(tree, dict):
        return types.SimpleNamespace(**{key: named(value) for key, value in tree.items()})
    if isinstance(tree, list):
        return [named(value) for value in tree]
    return tree


def split(value):
    high = value.astype(BF16)
    low = (value - high.astype(F32)).astype(BF16)
    return high, low


def kernel(*refs):
    leaf_rhs_ref, mid_rhs_ref, root_rhs_ref = refs[:3]
    matrix_refs = refs[3:13]
    parent_ref, sizes_ref, leaf_map_ref, mid_map_ref = refs[13:17]
    out_leaf, out_mid, out_root = refs[17:20]
    scratch = named(jax.tree.unflatten(TREE, refs[20 : 20 + len(SHAPES)]))
    send_sems, recv_sems, load_sems, out_sems = refs[20 + len(SHAPES) :]

    s = lax.axis_index("subtree")
    f = lax.axis_index("front")
    xi, yi = f // 4, f % 4
    zi, ci = s // 2, s % 2
    rank = ci * 8 + zi

    def device(dx=0, dy=0, dz=0, dc=0):
        return (
            ((zi + dz) % 8) * 2 + (ci + dc) % 2,
            ((xi + dx) % 4) * 4 + (yi + dy) % 4,
        )

    def load(index, src, dst):
        copy = pltpu.make_async_copy(src, dst, load_sems.at[index])
        copy.start()
        return copy

    load_leaf_rhs = load(10, leaf_rhs_ref, scratch.leaf_rhs)
    quarters = [pl.ds(512 * i, 512) for i in range(4)]
    firsts = [
        load(13 + i, matrix_refs[0].at[rows], scratch.raw[0].at[rows])
        for i, rows in enumerate(quarters)
    ]

    barrier = pltpu.get_barrier_semaphore()
    partners = [device(dx=d) for d in (1, 2, 3)] + [device(dy=d) for d in (1, 2, 3)]
    partners += [device(dz=d, dc=c) for d in range(8) for c in range(2) if (d, c) != (0, 0)]
    for partner in partners:
        pl.semaphore_signal(barrier, inc=1, device_id=partner, device_id_type=MESH)

    loads = []

    def load_rest():
        loads.extend([None] + [load(i, matrix_refs[i], scratch.raw[i]) for i in range(1, 10)])
        loads.append(load(11, mid_rhs_ref.at[:, rank], scratch.mid_rhs))
        loads.append(load(12, root_rhs_ref.at[:, rank], scratch.root_rhs))

    def cast(name):
        if name != LEAF_LOWER:
            loads[name].wait()
        src, dst = scratch.raw[name], scratch.split[name]
        width = src.shape[-1]
        if len(src.shape) == 3:

            def body(i, carry):
                high, low = split(src[i])
                dst[i, :, 0:width] = high
                dst[i, :, width : 2 * width] = low
                return carry

            lax.fori_loop(0, src.shape[0], body, 0)
        else:
            tile = 256 if width == 128 else 64

            def body(i, carry):
                rows = pl.ds(pl.multiple_of(i * tile, tile), tile)
                high, low = split(src[rows, :])
                dst[rows, 0:width] = high
                dst[rows, width : 2 * width] = low
                return carry

            lax.fori_loop(0, src.shape[0] // tile, body, 0)

    outputs, ready = [], []

    def output(index, src, dst):
        copy = pltpu.make_async_copy(src, dst, out_sems.at[index])
        copy.start()
        outputs.append(copy)

    counter = [0]
    first_send = [True]

    def chain(h):
        mine = scratch.chains[h]
        lanes = slice(h * LANES, (h + 1) * LANES)
        pending = []

        late = []

        def send(src, dst, target, kept=True):
            if first_send[0]:
                pl.semaphore_wait(barrier, len(partners))
                first_send[0] = False
            index = counter[0]
            counter[0] += 1
            copy = pltpu.make_async_remote_copy(
                src_ref=src,
                dst_ref=dst,
                send_sem=send_sems.at[index],
                recv_sem=recv_sems.at[index],
                device_id=target,
                device_id_type=MESH,
            )
            copy.start()
            (late if kept else pending).append(copy)
            return copy

        def flush():
            for copy in pending:
                copy.wait_send()
            pending.clear()

        def flush_late():
            for copy in late:
                copy.wait_send()
            late.clear()

        def arrive(copies):
            for copy in copies:
                copy.wait_recv()

        def put_x(row, value):
            depth = value.shape[0]
            high, low = split(value)
            x = mine.x
            for r in (row, row + depth):
                x[r : r + depth, 0:LANES] = high
                x[r : r + depth, LANES : 2 * LANES] = low

        def dot(a, b):
            both = jnp.dot(a, b, preferred_element_type=F32)
            return both[:, :LANES] + both[:, LANES:]

        def position(half):
            return (xi, yi) if half == 0 else (yi, xi)

        def along(half, primary, d):
            use_x = (half == 0) == primary
            return device(dx=d) if use_x else device(dy=d)

        def front_scatter(bufs, layout):
            part = mine.part

            def rows_of(half, to, upper):
                base, unit = layout[half]
                return pl.ds(pl.multiple_of(base + to * (4 * unit) + 2 * unit * upper, 8), 2 * unit)

            relayed, straight, summed = [], [], []
            for half, (base, unit) in enumerate(layout):
                ia, _ = position(half)
                copies = []
                for side, d in ((0, 1), (1, 3)):
                    rows = rows_of(half, (ia + 2) % 4, side)
                    copies.append(send(part.at[rows], bufs[half].relay.at[side], along(half, True, d), False))
                relayed.append(copies)
            for half, (base, unit) in enumerate(layout):
                ia, _ = position(half)
                copies = []
                for side, d in ((0, 1), (1, 3)):
                    rows = rows_of(half, (ia + d) % 4, 1 - side)
                    there = pl.ds(2 * unit * (1 - side), 2 * unit)
                    copies.append(
                        send(part.at[rows], bufs[half].r1.at[side, there], along(half, True, d), False)
                    )
                straight.append(copies)
            yield
            for half, (base, unit) in enumerate(layout):
                ia, _ = position(half)
                copies = []
                for side, d in ((0, 1), (1, 3)):
                    arrive([relayed[half][side]])
                    rows = rows_of(half, (ia + d) % 4, side)
                    part[rows, :] = part[rows, :] + bufs[half].relay[side]
                    there = pl.ds(2 * unit * side, 2 * unit)
                    copies.append(
                        send(part.at[rows], bufs[half].r1.at[side, there], along(half, True, d), False)
                    )
                summed.append(copies)
            yield
            second = []
            for half, (base, unit) in enumerate(layout):
                ia, ib = position(half)
                got = bufs[half].r1
                arrive(straight[half])
                arrive(summed[half])
                own = pl.multiple_of(base + ia * (4 * unit), 8)
                rows = pl.ds(own, 4 * unit)
                part[rows, :] = part[rows, :] + (got[0] + got[1])
                got2 = bufs[half].r2
                mineset = []
                for d in (2, 1, 3):
                    to = (ib + d) % 4
                    rows = pl.ds(pl.multiple_of(own + to * unit, 8), unit)
                    mineset.append(send(part.at[rows], got2.at[d - 1], along(half, False, d), False))
                second.append(mineset)
            yield
            sums = []
            for half, (base, unit) in enumerate(layout):
                ia, ib = position(half)
                got2 = bufs[half].r2
                arrive(second[half])
                rows = pl.ds(pl.multiple_of(base + ia * (4 * unit) + ib * unit, 8), unit)
                sums.append((part[rows, :] + got2[0]) + (got2[1] + got2[2]))
            return sums

        def front_reduce(bufs, layout, full, minuend=None):
            part = mine.part
            first = []
            for half, (base, unit) in enumerate(layout):
                ia, _ = position(half)
                copies = []
                for d in (2, 1, 3):
                    to = (ia + d) % 4
                    rows = pl.ds(pl.multiple_of(base + to * (4 * unit), 8), 4 * unit)
                    copies.append(send(part.at[rows], bufs[half].r1.at[d - 1], along(half, True, d), False))
                first.append(copies)
            yield
            second = []
            for half, (base, unit) in enumerate(layout):
                ia, ib = position(half)
                got, got2 = bufs[half].r1, bufs[half].r2
                arrive(first[half])
                rows = pl.ds(pl.multiple_of(base + ia * (4 * unit), 8), 4 * unit)
                got2[ib] = (part[rows, :] + got[0]) + (got[1] + got[2])
                second.append(
                    [send(got2.at[ib], got2.at[ib], along(half, False, d)) for d in (2, 1, 3)]
                )
            yield
            last = []
            for half, (base, unit) in enumerate(layout):
                ia, _ = position(half)
                got2 = bufs[half].r2
                arrive(second[half])
                rows = pl.ds(pl.multiple_of(base + ia * (4 * unit), 8), 4 * unit)
                total = (got2[0] + got2[1]) + (got2[2] + got2[3])
                full[rows, :] = total if minuend is None else minuend[rows, :] - total
                last.append(
                    [send(full.at[rows], full.at[rows], along(half, True, d)) for d in (2, 1, 3)]
                )
            yield
            for copies in last:
                arrive(copies)

        def subtree_scatter(bufs, zpart):
            got = bufs.core
            theirs = pl.ds(pl.multiple_of((1 - ci) * 8, 8), 8)
            copy = send(zpart.at[theirs], got, device(dc=1), False)
            yield
            arrive([copy])
            start = pl.multiple_of(ci * 8, 8)
            zpart[pl.ds(start, 8)] = zpart[pl.ds(start, 8)] + got[...]
            ring = bufs.ring
            copies = []
            for d in (4, 3, 5, 2, 6, 1, 7):
                to = (zi + d) % 8
                copies.append(send(zpart.at[start + to], ring.at[d - 1], device(dz=d), False))
            yield
            arrive(copies)
            a = (ring[0] + ring[1]) + (ring[2] + ring[3])
            b = (ring[4] + ring[5]) + (ring[6] + zpart[rank])
            return a + b

        def subtree_gather(full, chunk):
            full[rank] = chunk
            near = (1, 7, 2, 6, 3, 5, 4)
            copies = {d: send(full.at[rank], full.at[rank], device(dz=d)) for d in reversed(near)}
            across = [send(full.at[rank], full.at[rank], device(dc=1))]
            yield
            for d in near:
                arrive([copies[d]])
                slot = ci * 8 + (zi + 8 - d) % 8
                across.append(send(full.at[slot], full.at[slot], device(dc=1)))
            yield
            arrive(across)

        def leaf_product(name):
            flush()
            part = mine.part
            y = dot(scratch.split[name][...], mine.x[0:256, :])
            for block in range(16):
                low, high = block * 64, 1024 + ((block % 4) * 4 + block // 4) * 64
                part[low : low + 64, :] = y[block * 128 : block * 128 + 64]
                part[high : high + 64, :] = y[block * 128 + 64 : block * 128 + 128]

        def mid_product(name, across_subtree):
            flush()
            x, a = mine.x, scratch.split[name]
            for p in range(4):
                y = dot(a[p], x[512 * p : 512 * p + 512, :])
                if across_subtree:
                    y = y.reshape(2, 16, 8, LANES)
                    mine.zpart8[:, 2 * p] = y[0]
                    mine.zpart8[:, 2 * p + 1] = y[1]
                else:
                    mine.part[256 * p : 256 * p + 256, :] = y

        def root_product(name, across_subtree):
            flush()
            y = dot(scratch.split[name][...], mine.x[0:1280, :])
            if across_subtree:
                for q in range(5):
                    mine.zpart5[:, q] = y[128 * q : 128 * q + 128].reshape(16, 8, LANES)
            else:
                mine.part[0:640, :] = y

        def block_of(full, t):
            return full[:, t].reshape(128, LANES)

        def root_slot(p, k):
            return jnp.clip(mid_map_ref[p, 2 * f + k] - 5 * f, 0, 4)

        positions = f * 128 + lax.broadcasted_iota(jnp.int32, (128, LANES), 0)
        live = (positions < sizes_ref[s]).astype(F32)
        lead = h == 0

        if lead:
            load_leaf_rhs.wait()
            for copy in firsts:
                copy.wait()
            cast(LEAF_LOWER)
        put_x(0, live * scratch.leaf_rhs[:, lanes])
        leaf_product(LEAF_LOWER)
        stage = front_scatter(mine.p1, FRONT_LEAF)
        next(stage)
        if lead:
            load_rest()
            cast(LEAF_BELOW)
        yield
        sums = yield from stage
        leaf_fwd = live * jnp.concatenate(sums, axis=0)
        mine.leaf_fwd[...] = leaf_fwd

        put_x(0, leaf_fwd)
        leaf_product(LEAF_BELOW)
        stage = front_scatter(mine.p2, FRONT_LEAF)
        next(stage)
        if lead:
            cast(MID_LOWER)
        yield
        sums = yield from stage
        contrib = -jnp.concatenate(sums, axis=0)

        mine.contrib[...] = contrib.reshape(16, 8, LANES)
        children = mine.children
        children[s] = mine.contrib[rank]
        copies = []
        for d in (4, 3, 5, 2, 6, 1, 7, 0):
            for c in range(2):
                if (d, c) != (0, 0):
                    to = ((ci + c) % 2) * 8 + (zi + d) % 8
                    copies.append(send(mine.contrib.at[to], children.at[s], device(dz=d, dc=c)))
        if lead:
            cast(MID_BELOW)
            loads[10].wait()
        yield
        arrive(copies)
        placed = [jnp.zeros((8, LANES), F32) for _ in range(16)]
        for g in range(16):
            block = leaf_map_ref[g, f]
            upper = block >= 32
            slot = block - 2 * f - jnp.where(upper, 32, 0)
            target = parent_ref[g] * 4 + jnp.where(upper, 2, 0) + slot
            value = children[g]
            for t in range(16):
                placed[t] = placed[t] + jnp.where(target == t, value, 0.0)
        rhs = scratch.mid_rhs
        pivot = [rhs[t, :, lanes] + placed[(t // 2) * 4 + t % 2] for t in range(8)]
        mine.update[...] = jnp.stack([placed[(t // 2) * 4 + 2 + t % 2] for t in range(8)])
        yield from subtree_gather(mine.pivot, jnp.stack(pivot))

        for p in range(4):
            full = mine.pivot
            put_x(512 * p, jnp.concatenate([block_of(full, 2 * p), block_of(full, 2 * p + 1)], axis=0))
        mid_product(MID_LOWER, False)
        stage = front_reduce(mine.x4, FRONT_MID, mine.mid_fwd)
        next(stage)
        if lead:
            cast(ROOT_LOWER)
        yield
        yield from stage

        for p in range(4):
            put_x(512 * p, mine.mid_fwd[256 * p : 256 * p + 256, :])
        mid_product(MID_BELOW, True)
        stage = subtree_scatter(mine.z5, mine.zpart8)
        next(stage)
        yield
        next(stage)
        if lead:
            cast(ROOT_UPPER)
            loads[11].wait()
        yield
        chunk = mine.update[...] - (yield from stage)
        start = [scratch.root_rhs[q, :, lanes] for q in range(5)]
        for p in range(4):
            for k in range(2):
                slot = mid_map_ref[p, 2 * f + k] - 5 * f
                for q in range(5):
                    start[q] = start[q] + jnp.where(slot == q, chunk[2 * p + k], 0.0)
        yield from subtree_gather(mine.start, jnp.stack(start))

        put_x(0, jnp.concatenate([block_of(mine.start, q) for q in range(5)], axis=0))
        root_product(ROOT_LOWER, False)
        stage = front_reduce(mine.x6, FRONT_ROOT, mine.root_fwd)
        next(stage)
        if lead:
            cast(MID_RIGHT)
        yield
        yield from stage

        put_x(0, mine.root_fwd[...])
        root_product(ROOT_UPPER, True)
        stage = subtree_scatter(mine.z7, mine.zpart5)
        next(stage)
        yield
        next(stage)
        if lead:
            cast(MID_UPPER)
        yield
        chunk = yield from stage
        yield from subtree_gather(mine.root_sol, chunk)

        for p in range(4):
            ext = [
                block_of(mine.root_sol, root_slot(p, k)) for k in range(2)
            ]
            put_x(512 * p, jnp.concatenate(ext, axis=0))
        mid_product(MID_RIGHT, False)
        stage = front_reduce(mine.x8, FRONT_MID, mine.mid_back, mine.mid_fwd)
        next(stage)
        if lead:
            cast(LEAF_RIGHT)
        for q in range(5):
            scratch.out_root[q, :, :, lanes] = mine.root_sol[:, q]
        ready.append(8)
        if ready.count(8) == 2:
            output(2, scratch.out_root, out_root)
        yield
        yield from stage

        for p in range(4):
            put_x(512 * p, mine.mid_back[256 * p : 256 * p + 256, :])
        mid_product(MID_UPPER, True)
        stage = subtree_scatter(mine.z9, mine.zpart8)
        next(stage)
        yield
        next(stage)
        if lead:
            cast(LEAF_UPPER)
        yield
        mine.mid_own[...] = yield from stage

        def leaf_target(g):
            block = leaf_map_ref[g, f]
            upper = block >= 32
            return parent_ref[g], jnp.clip(block - 2 * f - jnp.where(upper, 32, 0), 0, 1), upper

        for g in range(16):
            p, slot, _ = leaf_target(g)
            mine.picked[g] = mine.mid_own[2 * p + slot]
        mine.leaf_ext[rank] = mine.picked[s]
        copies = []
        for d in (4, 3, 5, 2, 6, 1, 7, 0):
            for c in range(2):
                if (d, c) != (0, 0):
                    to = ((zi + d) % 8) * 2 + (ci + c) % 2
                    copies.append(
                        send(mine.picked.at[to], mine.leaf_ext.at[rank], device(dz=d, dc=c))
                    )
        gather = subtree_gather(mine.mid_sol, mine.mid_own[...])
        next(gather)
        yield
        arrive(copies)

        p, slot, upper = leaf_target(s)
        from_sol = mine.leaf_ext[...].reshape(128, LANES)
        from_ext = block_of(mine.root_sol, root_slot(p, slot))
        put_x(0, jnp.where(upper, from_ext, from_sol))
        leaf_product(LEAF_RIGHT)
        stage = front_scatter(mine.p10, FRONT_LEAF)
        next(stage)
        yield
        next(stage)
        next(gather)
        yield
        sums = yield from stage
        put_x(0, live * (mine.leaf_fwd[...] - jnp.concatenate(sums, axis=0)))

        leaf_product(LEAF_UPPER)
        stage = front_scatter(mine.p11, FRONT_LEAF)
        next(stage)
        next(gather, None)
        for t in range(8):
            scratch.out_mid[t, :, :, lanes] = mine.mid_sol[:, t]
        ready.append(10)
        if ready.count(10) == 2:
            output(1, scratch.out_mid, out_mid)
        flush_late()
        yield
        sums = yield from stage
        scratch.out_leaf[:, lanes] = live * jnp.concatenate(sums, axis=0)
        flush()
        flush_late()

    chains = [chain(0), chain(1)]
    for which in ORDER:
        next(chains[which], None)

    output(0, scratch.out_leaf, out_leaf)
    for copy in outputs:
        copy.wait()


def copy_kernel(a, b, c, a_out, b_out, c_out, a_held, b_held, c_held, sems):
    steps = ((b, b_held, b_out), (c, c_held, c_out), (a, a_held, a_out))
    reads = [pltpu.make_async_copy(x, y, sems.at[i]) for i, (x, y, _) in enumerate(steps)]
    writes = [pltpu.make_async_copy(y, z, sems.at[3 + i]) for i, (_, y, z) in enumerate(steps)]
    for copy in reads:
        copy.start()
    for read, write in zip(reads, writes):
        read.wait()
        write.start()
    for copy in writes:
        copy.wait()


def on_device(
    leaf_rhs,
    mid_rhs,
    root_rhs,
    leaf_lower,
    leaf_below,
    leaf_right,
    leaf_upper,
    mid_lower,
    mid_below,
    mid_right,
    mid_upper,
    root_lower,
    root_upper,
    leaf_parent,
    leaf_sizes,
    leaf_map,
    mid_map,
):
    operands = [leaf_rhs[0], mid_rhs.reshape(8, 16, 8, 256), root_rhs.reshape(5, 16, 8, 256)]
    operands += [leaf_lower[0], leaf_below[0], mid_lower, mid_below, root_lower]
    operands += [root_upper, mid_right, mid_upper, leaf_right[0], leaf_upper[0]]
    anywhere = pl.BlockSpec(memory_space=pl.ANY)
    scalars = pl.BlockSpec(memory_space=pltpu.SMEM)
    shapes = (
        jax.ShapeDtypeStruct((128, 256), F32),
        jax.ShapeDtypeStruct((8, 16, 8, 256), F32),
        jax.ShapeDtypeStruct((5, 16, 8, 256), F32),
    )
    results = pl.pallas_call(
        kernel,
        out_shape=shapes,
        in_specs=[anywhere] * len(operands) + [scalars] * 4,
        out_specs=(anywhere,) * 3,
        scratch_shapes=SHAPES
        + [
            pltpu.SemaphoreType.DMA((SEMS,)),
            pltpu.SemaphoreType.DMA((SEMS,)),
            pltpu.SemaphoreType.DMA((17,)),
            pltpu.SemaphoreType.DMA((3,)),
        ],
        compiler_params=pltpu.CompilerParams(
            collective_id=0, has_side_effects=True, vmem_limit_bytes=60 * 2**20
        ),
        name="solve",
    )(*operands, leaf_parent, leaf_sizes, leaf_map, mid_map)
    leaf_sol, mid_sol, root_sol = pl.pallas_call(
        copy_kernel,
        out_shape=shapes,
        in_specs=[anywhere] * 3,
        out_specs=(anywhere,) * 3,
        scratch_shapes=[pltpu.VMEM(shape.shape, F32) for shape in shapes]
        + [pltpu.SemaphoreType.DMA((6,))],
    )(*results)
    return leaf_sol[None], mid_sol.reshape(4, 256, 256), root_sol.reshape(640, 256)


def solution(mesh):
    return jax.shard_map(
        on_device,
        mesh=mesh,
        in_specs=(
            P("subtree", "front", None),
            P(None, "front", None),
            P("front", None),
            P("subtree", None, "front"),
            P("subtree", None, "front"),
            P("subtree", None, "front"),
            P("subtree", None, "front"),
            P(None, "subtree", "front"),
            P(None, "front", "subtree"),
            P(None, "subtree", "front"),
            P(None, "front", "subtree"),
            P("subtree", "front"),
            P("front", "subtree"),
            P(),
            P(),
            P(),
            P(),
        ),
        out_specs=(P("subtree", "front", None), P(None, "front", None), P("front", None)),
        check_vma=False,
    )
```
